32 devices in a mesh: own: 2 (over y), space: 16 (over z, x, core).
Axes of the slice: x: 2, y: 2, z: 4, core: 2. Of those that a mesh axis runs over, the one named last changes fastest.
Arguments:
- density: bfloat16 [256, 4, 64, 128], P(None, 'own', 'space'), may hold values from -6 to 6
- cotangent: bfloat16 [256, 4, 64, 128], P(None, 'own', 'space'), may hold values from -6 to 6
- pw_one: bfloat16 [256, 256], P('own'), may hold values from -0.375 to 0.375
- pw_two: bfloat16 [256, 256], P('own'), may hold values from -0.375 to 0.375
- dw_one: bfloat16 [27, 256], P(None, 'own'), may hold values from -1.25 to 1.25
- dw_two: bfloat16 [27, 256], P(None, 'own'), may hold values from -1.25 to 1.25
Outputs:
- grad_input: bfloat16 [256, 4, 64, 128], P(None, 'own', 'space')
- grad_pw_one: float32 [256, 256], P('own')
- grad_pw_two: float32 [256, 256], P('own')
- grad_dw_one: float32 [27, 256], P(None, 'own')
- grad_dw_two: float32 [27, 256], P(None, 'own')
The draws below stay inside these ranges and needn't reach their ends.
All inputs are finite; a program needn't handle non-finite values.
Results may differ from the reference program's by a relative error of at most 0.01.
Values may be sent and summed in bfloat16 or wider, within the bound.
No kernel may reach another device: no remote copies, remote signals or barrier semaphores. Data moves between devices by JAX's collectives and lax.ppermute only.
A program may use at most 192 MiB of HBM per device.

```python
import math
import jax
import jax.numpy as jnp
from jax import lax

C = 256
NX = 4
NY = 64
NZ = 128


def shard_levels(own_key, dims, split, smallest, top_value):
    level = 1.0
    for dim, shards_of in split:
        heights = jax.random.uniform(jax.random.fold_in(jax.random.fold_in(own_key, 6), dim), (shards_of,), jnp.float32, smallest / len(split), top_value / len(split))
        level = level * jnp.repeat(jnp.exp(heights), dims[dim] // shards_of).reshape((-1,) + (1,) * (len(dims) - 1 - dim))
    return level


def centred(stream_key, shape, deviation, most, split=(), held_as=jnp.bfloat16):
    loudness = shard_levels(stream_key, shape, split, -0.22, 0.18) if split else 1.0
    array = jax.random.normal(stream_key, shape, jnp.float32) * deviation * loudness
    return jnp.minimum(jnp.maximum(array, -most), most).astype(held_as)


def setup_inputs(seed: int = 0) -> dict:
    key_list = jax.random.split(jax.random.key(seed), 7)
    return {
        "density": centred(key_list[0], (C, NX, NY, NZ), 1.0, 6.0, ((1, 2), (2, 16))),
        "cotangent": centred(key_list[1], (C, NX, NY, NZ), 1.0, 6.0, ((1, 2), (2, 16))),
        "pw_one": centred(key_list[2], (C, C), C ** -0.5, 0.375, ((0, 2),)),
        "pw_two": centred(key_list[3], (C, C), C ** -0.5, 0.375, ((0, 2),)),
        "dw_one": centred(key_list[4], (27, C), 27 ** -0.5, 1.25, ((1, 2),)),
        "dw_two": centred(key_list[5], (27, C), 27 ** -0.5, 1.25, ((1, 2),)),
    }


TAP_LIST = [(9 * (a + 1) + 3 * (b + 1) + (d + 1), a, b, d) for a in (-1, 0, 1) for b in (-1, 0, 1) for d in (-1, 0, 1)]

def depthwise_ref(source, weights, direction):
    groups = C // 16

    def per_group(operands):
        channel_block, weight_block = operands
        running = jnp.zeros(channel_block.shape, jnp.float32)
        for k, a, b, d in TAP_LIST:
            shifted = jnp.roll(channel_block, (-direction * a, -direction * b, -direction * d), (1, 2, 3))
            running = running + weight_block[:, k].astype(jnp.float32)[:, None, None, None] * shifted.astype(jnp.float32)
        return running
    output = lax.map(per_group, (source.reshape(groups, 16, NX, NY, NZ), weights.T.reshape(groups, 16, 27)))
    return output.reshape(C, NX, NY, NZ)

def tap_ref(source, gradient):
    groups = C // 16

    def per_group(operands):
        channel_block, grad_block = operands
        grad_float = grad_block.astype(jnp.float32)
        columns = []
        for k, a, b, d in TAP_LIST:
            shifted = jnp.roll(channel_block, (-a, -b, -d), (1, 2, 3)).astype(jnp.float32)
            columns.append(lax.optimization_barrier(jnp.sum(shifted * grad_float, axis=(1, 2, 3))))
        return jnp.stack(columns, axis=1)
    output = lax.map(per_group, (source.reshape(groups, 16, NX, NY, NZ), gradient.reshape(groups, 16, NX, NY, NZ)))
    return output.reshape(C, 27).T

def contract_cells(left, right):
    return lax.dot_general(left.reshape(C, -1), right.reshape(C, -1), (((1,), (1,)), ((), ())), preferred_element_type=jnp.float32)

def reference(density, cotangent, pw_one, pw_two, dw_one, dw_two):
    grad_scale = 1.0 / math.sqrt(float(NX * NY * NZ))
    first = depthwise_ref(density, dw_one, 1).astype(jnp.bfloat16)
    pre = jnp.dot(pw_one.T, first.reshape(C, -1), preferred_element_type=jnp.float32).reshape(C, NX, NY, NZ)
    act = jax.nn.silu(pre).astype(jnp.bfloat16)
    second = depthwise_ref(act, dw_two, 1).astype(jnp.bfloat16)
    grad_second = jnp.dot(pw_two, cotangent.reshape(C, -1), preferred_element_type=jnp.float32).reshape(C, NX, NY, NZ).astype(jnp.bfloat16)
    sigma = jax.nn.sigmoid(pre)
    grad_pre = (depthwise_ref(grad_second, dw_two, -1) * (sigma * (1.0 + pre * (1.0 - sigma)))).astype(jnp.bfloat16)
    grad_first = jnp.dot(pw_one, grad_pre.reshape(C, -1), preferred_element_type=jnp.float32).reshape(C, NX, NY, NZ).astype(jnp.bfloat16)
    grad_input = (cotangent.astype(jnp.float32) + depthwise_ref(grad_first, dw_one, -1)).astype(jnp.bfloat16)
    grad_pw_two = contract_cells(second, cotangent) * grad_scale
    grad_pw_one = contract_cells(first, grad_pre) * grad_scale
    grad_dw_two = tap_ref(act, grad_second) * grad_scale
    grad_dw_one = tap_ref(density, grad_first) * grad_scale
    return (grad_input, grad_pw_one, grad_pw_two, grad_dw_one, grad_dw_two)
```

```python
import functools
import math

import jax
import jax.numpy as jnp
from jax import lax
from jax.experimental import pallas as pl
from jax.experimental.pallas import tpu as pltpu
from jax.sharding import PartitionSpec as P

AXES = ("own", "space")
BF = jnp.bfloat16
F32 = jnp.float32
TAPS = [
    (9 * (a + 1) + 3 * (b + 1) + (d + 1), a, b, d)
    for a in (-1, 0, 1)
    for b in (-1, 0, 1)
    for d in (-1, 0, 1)
]
LANES = 128
GROUP = 16
VMEM = pl.BlockSpec(memory_space=pltpu.VMEM)
SMEM = pl.BlockSpec(memory_space=pltpu.SMEM)


def tree(terms):
    while len(terms) > 1:
        paired = [terms[i] + terms[i + 1] for i in range(0, len(terms) - 1, 2)]
        terms = paired + ([terms[-1]] if len(terms) % 2 else [])
    return terms[0]


def turned(value, shift):
    return pltpu.roll(value, shift % LANES, 1)


def conv_rows(load, weights, planes, rows, direction, emit):
    for x in range(planes):
        for y in rows:
            parts = {-1: [], 0: [], 1: []}
            for k, a, b, d in TAPS:
                parts[d].append(weights[k] * load((x + direction * a) % planes, y + direction * b))
            total = tree(parts[0]).astype(F32)
            total = total + turned(tree(parts[1]).astype(F32), -direction)
            total = total + turned(tree(parts[-1]).astype(F32), direction)
            emit(x, y, total)


def tap_products(load, gradient, planes, rows, emit):
    turns = {}
    for x in range(planes):
        for y in rows:
            value = gradient(x, y)
            wide = value.astype(F32)
            turns[x, y] = {-1: turned(wide, -1).astype(BF), 0: value, 1: turned(wide, 1).astype(BF)}
    for k, a, b, d in TAPS:
        emit(k, tree([load((x + a) % planes, y + b) * turns[x, y][d] for x in range(planes) for y in rows]))


def side_by_side(slabs):
    return jnp.concatenate(slabs, axis=1)


def channel_groups(body, channels):
    def step(group, carry):
        body(pl.ds(pl.multiple_of(group * GROUP, GROUP), GROUP))
        return carry

    lax.fori_loop(0, channels // GROUP, step, 0)


def contract(left, right):
    return lax.dot_general(left, right, (((1,), (1,)), ((), ())), preferred_element_type=F32)


def fill_extended(own, ext, local, beside, strip, rest, halo, halo_beside, height):
    del strip
    span = height + 2
    for x in range(2):
        for y in range(height):
            ext[x * span + 2 * (1 - own) + y] = local[x * height + y]
        for y in range(2):
            ext[x * span + 4 * own + y] = halo[x * 2 + y]
            ext[(x + 2) * span + 4 * own + y] = halo_beside[x * 2 + y]
            ext[(x + 2) * span + 2 + y] = beside[x * 2 + y]
            ext[(x + 2) * span + 4 * (1 - own) + y] = rest[x * 2 + y]


def forward_kernel(own_ref, local, beside, rest, halo, halo_beside, taps, weight_t, ext, first, act, slope):
    own = own_ref[0]
    channels = local.shape[1]
    fill_extended(own, ext, local, beside, None, rest, halo, halo_beside, 4)

    def group(rows):
        weights = [taps[k, rows, :] for k in range(27)]

        def emit(x, y, total):
            first[x * 4 + y - 1, rows, :] = total.astype(BF)

        conv_rows(lambda x, y: ext[x * 6 + y, rows, :], weights, 4, range(1, 5), 1, emit)

    channel_groups(group, channels)

    def pointwise(step, carry):
        base = step * 4
        source = side_by_side([first[base + j] for j in range(4)])
        pre = jnp.dot(weight_t[...], source, preferred_element_type=F32)
        sigma = jax.nn.sigmoid(pre)
        value = (pre * sigma).astype(BF)
        factor = (sigma * (1.0 + pre * (1.0 - sigma))).astype(BF)
        for j in range(4):
            act[base + j] = value[:, j * LANES : (j + 1) * LANES]
            slope[base + j] = factor[:, j * LANES : (j + 1) * LANES]
        return carry

    lax.fori_loop(0, 4, pointwise, 0)


def second_kernel(own_ref, act, local, beside, taps, weight, selector, grad_pw, grad_dw, second, grad_second, cotan, products):
    own = own_ref[0]
    channels = act.shape[1]
    for x in range(2):
        for y in range(2):
            cotan[x * 2 + y] = local[x * 4 + 2 * own + y]
            cotan[(x + 2) * 2 + y] = beside[x * 2 + y]
    for x in range(4):
        source = side_by_side([cotan[x * 2], cotan[x * 2 + 1]])
        value = jnp.dot(weight[...], source, preferred_element_type=F32).astype(BF)
        grad_second[x * 2] = value[:, :LANES]
        grad_second[x * 2 + 1] = value[:, LANES:]

    def group(rows):
        weights = [taps[k, rows, :] for k in range(27)]
        load = lambda x, y: act[x * 4 + y, rows, :]

        def emit(x, y, total):
            second[x * 2 + y - 1, rows, :] = total.astype(BF)

        conv_rows(load, weights, 4, range(1, 3), 1, emit)

        def keep(k, value):
            products[rows, k * LANES : (k + 1) * LANES] = value

        tap_products(load, lambda x, y: grad_second[x * 2 + y - 1, rows, :], 4, range(1, 3), keep)

    channel_groups(group, channels)
    total = jnp.zeros((channels, channels), F32)
    for x in range(4):
        total += contract(side_by_side([second[2 * x], second[2 * x + 1]]), side_by_side([cotan[2 * x], cotan[2 * x + 1]]))
    grad_pw[...] = total
    grad_dw[...] = jnp.dot(products[...], selector[...], preferred_element_type=F32)


def backward_kernel(
    own_ref, local, beside, rest, halo, halo_beside, slope, first, density, taps, weight_two, weight_one, selector,
    grad_first, grad_pw, grad_dw, ext, grad_second, grad_pre, products,
):
    own = own_ref[0]
    channels = local.shape[1]
    fill_extended(own, ext, local, beside, None, rest, halo, halo_beside, 4)

    def pointwise(step, carry):
        source = side_by_side([ext[step * 4 + j] for j in range(4)])
        value = jnp.dot(weight_two[...], source, preferred_element_type=F32).astype(BF)
        for j in range(4):
            grad_second[step * 4 + j] = value[:, j * LANES : (j + 1) * LANES]
        return carry

    lax.fori_loop(0, 6, pointwise, 0)

    def group(rows):
        weights = [taps[k, rows, :] for k in range(27)]

        def emit(x, y, total):
            slab = x * 4 + y - 1
            grad_pre[slab, rows, :] = (total * slope[slab, rows, :].astype(F32)).astype(BF)

        conv_rows(lambda x, y: grad_second[x * 6 + y, rows, :], weights, 4, range(1, 5), -1, emit)

    channel_groups(group, channels)

    def backmap(step, carry):
        source = side_by_side([grad_pre[step * 4 + j] for j in range(4)])
        value = jnp.dot(weight_one[...], source, preferred_element_type=F32).astype(BF)
        for j in range(4):
            grad_first[step * 4 + j] = value[:, j * LANES : (j + 1) * LANES]
        return carry

    lax.fori_loop(0, 4, backmap, 0)
    total = jnp.zeros((channels, channels), F32)
    for x in range(4):
        total += contract(
            side_by_side([first[4 * x + 1], first[4 * x + 2]]), side_by_side([grad_pre[4 * x + 1], grad_pre[4 * x + 2]])
        )
    grad_pw[...] = total

    def tap_group(rows):
        def keep(k, value):
            products[rows, k * LANES : (k + 1) * LANES] = value

        tap_products(
            lambda x, y: density[x * 6 + y, rows, :], lambda x, y: grad_first[x * 4 + y - 1, rows, :], 4, range(2, 4), keep
        )

    channel_groups(tap_group, channels)
    grad_dw[...] = jnp.dot(products[...], selector[...], preferred_element_type=F32)


def input_kernel(own_ref, local, beside, grad_first, taps, mine, other):
    own = own_ref[0]
    channels = local.shape[1]

    def group(rows):
        weights = [taps[k, rows, :] for k in range(27)]

        def emit(x, y, total):
            slab = (x % 2) * 2 + y - 1
            if x < 2:
                mine[slab, rows, :] = (local[x * 4 + 2 * own + y - 1, rows, :].astype(F32) + total).astype(BF)
            else:
                other[slab, rows, :] = (beside[slab, rows, :].astype(F32) + total).astype(BF)

        conv_rows(lambda x, y: grad_first[x * 4 + y, rows, :], weights, 4, range(1, 3), -1, emit)

    channel_groups(group, channels)


def call(kernel, name, outs, scratch, inputs, flops):
    return pl.pallas_call(
        kernel,
        name=name,
        out_shape=[jax.ShapeDtypeStruct(shape, dtype) for shape, dtype in outs],
        in_specs=[SMEM] + [VMEM] * (len(inputs) - 1),
        out_specs=[VMEM] * len(outs),
        scratch_shapes=[pltpu.VMEM(shape, dtype) for shape, dtype in scratch],
        compiler_params=pltpu.CompilerParams(vmem_limit_bytes=48 * 1024 * 1024),
        cost_estimate=pl.CostEstimate(flops=flops, bytes_accessed=4 * 1024 * 1024, transcendentals=0),
    )(*inputs)


def shards(density, cotangent, pw_one, pw_two, dw_one, dw_two):
    channels, extent_x, extent_y, extent_z = density.shape
    own_size, space_size = lax.axis_size("own"), lax.axis_size("space")
    own = lax.axis_index("own")
    place = lambda o, s: o * space_size + s % space_size
    every = [(o, s) for o in range(own_size) for s in range(space_size)]
    across = [(place(o, s), place(1 - o, s)) for o, s in every]
    onward = [(place(o, s), place(o, s + 1 - 2 * o)) for o, s in every]
    swap = lambda value: lax.ppermute(value, AXES, across)
    pass_on = lambda value: lax.ppermute(value, AXES, onward)
    slabs = 2 * extent_x
    own_ref = own.astype(jnp.int32).reshape(1)

    def gathered(value, axis):
        other = swap(value)
        return jnp.where(own == 0, jnp.concatenate([value, other], axis), jnp.concatenate([other, value], axis))

    def pieces(value):
        rows = value.transpose(1, 2, 0, 3)
        strip = lax.dynamic_slice_in_dim(rows, 2 * own, 2, 1).reshape(slabs, channels, extent_z)
        rest = lax.dynamic_slice_in_dim(rows, 2 - 2 * own, 2, 1).reshape(slabs, channels, extent_z)
        return rows.reshape(extent_x * extent_y, channels, extent_z), strip, rest

    dw_both = gathered(jnp.concatenate([dw_one, dw_two], 0), 1)
    density_rows, density_strip, density_rest = pieces(density)
    density_far = swap(density_strip)
    density_beside = swap(density_rest)
    density_halo = pass_on(density_rest)
    density_halo_far = pass_on(density_far)
    pw_both = gathered(jnp.stack([pw_one, pw_two]), 1)
    cot_rows, cot_strip, cot_rest = pieces(cotangent)
    cot_far = swap(cot_strip)
    cot_beside = swap(cot_rest)
    cot_halo = pass_on(cot_rest)
    cot_halo_far = pass_on(cot_far)

    taps_one = jnp.broadcast_to(dw_both[:27, :, None], (27, channels, LANES))
    taps_two = jnp.broadcast_to(dw_both[27:, :, None], (27, channels, LANES))
    weight_one, weight_two = pw_both[0], pw_both[1]
    selector = (lax.broadcasted_iota(jnp.int32, (27 * LANES, LANES), 0) // LANES == lax.broadcasted_iota(jnp.int32, (27 * LANES, LANES), 1)).astype(BF)

    slab = (channels, LANES)
    density_ext, first, act, slope = call(
        forward_kernel, "forward",
        [((24,) + slab, BF), ((16,) + slab, BF), ((16,) + slab, BF), ((16,) + slab, BF)], [],
        (own_ref, density_rows, density_beside, density_far, density_halo, density_halo_far, taps_one, weight_one.T),
        5_000_000_000,
    )
    pw_two_part, dw_two_part = call(
        second_kernel, "second",
        [((channels, channels), F32), ((channels, LANES), F32)],
        [((8,) + slab, BF), ((8,) + slab, BF), ((8,) + slab, BF), ((channels, 27 * LANES), BF)],
        (own_ref, act, cot_rows, cot_beside, taps_two, weight_two, selector),
        5_000_000_000,
    )
    grad_first, pw_one_part, dw_one_part = call(
        backward_kernel, "backward",
        [((16,) + slab, BF), ((channels, channels), F32), ((channels, LANES), F32)],
        [((24,) + slab, BF), ((24,) + slab, BF), ((16,) + slab, BF), ((channels, 27 * LANES), BF)],
        (own_ref, cot_rows, cot_beside, cot_far, cot_halo, cot_halo_far, slope, first, density_ext, taps_two, weight_two, weight_one, selector),
        5_000_000_000,
    )
    mine, other = call(
        input_kernel, "input",
        [((4,) + slab, BF), ((4,) + slab, BF)], [],
        (own_ref, cot_rows, cot_beside, grad_first, taps_one),
        3_000_000_000,
    )

    def summed(pw_part, dw_part):
        half = channels // 2
        both = jnp.concatenate([pw_part, dw_part], 1).astype(BF)
        keep = lax.dynamic_slice_in_dim(both, own * half, half, 0)
        give = lax.dynamic_slice_in_dim(both, half - own * half, half, 0)
        total = keep.astype(F32) + swap(give).astype(F32)
        step = 1
        while step < space_size:
            pairs = [(place(o, s), place(o, s ^ step)) for o, s in every]
            sent = total.astype(BF)
            total = sent.astype(F32) + lax.ppermute(sent, AXES, pairs).astype(F32)
            step *= 2
        total = total * (1.0 / math.sqrt(float(extent_x * extent_y * extent_z * own_size * space_size)))
        return total[:, :channels], total[:, channels : channels + 27].T

    grad_pw_two, grad_dw_two = summed(pw_two_part, dw_two_part)
    grad_pw_one, grad_dw_one = summed(pw_one_part, dw_one_part)
    back = swap(other)
    mine = mine.reshape(2, 2, channels, extent_z)
    back = back.reshape(2, 2, channels, extent_z)
    rows = jnp.where(own == 0, jnp.concatenate([mine, back], 1), jnp.concatenate([back, mine], 1))
    grad_input = rows.transpose(2, 0, 1, 3)
    return grad_input, grad_pw_one, grad_pw_two, grad_dw_one, grad_dw_two


def solution(mesh):
    in_specs = (
        P(None, "own", "space", None),
        P(None, "own", "space", None),
        P("own", None),
        P("own", None),
        P(None, "own"),
        P(None, "own"),
    )
    out_specs = (
        P(None, "own", "space", None),
        P("own", None),
        P("own", None),
        P(None, "own"),
        P(None, "own"),
    )
    return jax.shard_map(shards, mesh=mesh, in_specs=in_specs, out_specs=out_specs, check_vma=False)
```

```python
import math

import jax
import jax.numpy as jnp
from jax import lax
from jax.experimental import pallas as pl
from jax.experimental.pallas import tpu as pltpu
from jax.sharding import PartitionSpec as P

AXES = ("own", "space")
BF = jnp.bfloat16
F32 = jnp.float32
TAPS = [
    (9 * (a + 1) + 3 * (b + 1) + (d + 1), a, b, d)
    for a in (-1, 0, 1)
    for b in (-1, 0, 1)
    for d in (-1, 0, 1)
]
LANES = 128
GROUP = 16
MICROSECONDS = {"density": 1, "cotangent": 1, "weights": 1, "stencils": 5, "forward": 5, "second": 4, "backward": 8, "input": 3, "finish": 1}
PLANES = 4
VMEM = pl.BlockSpec(memory_space=pltpu.VMEM)
SMEM = pl.BlockSpec(memory_space=pltpu.SMEM)
HBM = pl.BlockSpec(memory_space=pltpu.HBM)


def tap_index(a, b, d):
    return 9 * (a + 1) + 3 * (b + 1) + (d + 1)


def tree(terms):
    while len(terms) > 1:
        paired = [terms[i] + terms[i + 1] for i in range(0, len(terms) - 1, 2)]
        terms = paired + ([terms[-1]] if len(terms) % 2 else [])
    return terms[0]


def turned(value, shift):
    return pltpu.roll(value, shift % LANES, 1)


def side_by_side(slabs):
    return jnp.concatenate(slabs, axis=1)


def contract(left, right):
    return lax.dot_general(left, right, (((1,), (1,)), ((), ())), preferred_element_type=F32)


def group_rows(group):
    return pl.ds(group * GROUP, GROUP)


def stencil_sums(data, stencil, turn, moved, blocks, emit):
    height = 2 * blocks + 2
    for slab in range(PLANES * height):
        both = jnp.dot(data[slab], turn[...], preferred_element_type=F32).astype(BF)
        moved[0, slab] = both[:, :LANES]
        moved[1, slab] = both[:, LANES:]
    for group in range(data.shape[1] // GROUP):
        rows = group_rows(group)

        def piece(d, x, y):
            return data[x * height + y, rows, :] if d == 1 else moved[d // 2, x * height + y, rows, :]

        columns = [
            jnp.concatenate([piece(d, x, 2 * block + y) for d in range(3) for x in range(PLANES) for y in range(4)], axis=0)
            for block in range(blocks)
        ]
        total = jnp.dot(stencil[group], side_by_side(columns), preferred_element_type=F32)
        for x in range(PLANES):
            for block in range(blocks):
                for y in range(2):
                    start = (x * 2 + y) * GROUP
                    emit(x, 2 * block + y, rows, total[start : start + GROUP, block * LANES : (block + 1) * LANES])


def tap_products(load, gradient, rows, emit):
    turns = {}
    for x in range(PLANES):
        for y in rows:
            value = gradient(x, y)
            wide = value.astype(F32)
            turns[x, y] = {-1: turned(wide, -1).astype(BF), 0: value, 1: turned(wide, 1).astype(BF)}
    for k, a, b, d in TAPS:
        emit(k, tree([load((x + a) % PLANES, y + b) * turns[x, y][d] for x in range(PLANES) for y in rows]))


def tap_sums(load, gradient, rows, products, selector):
    channels = products.shape[0]

    def step(group, carry):
        at = pl.ds(pl.multiple_of(group * GROUP, GROUP), GROUP)

        def keep(k, value):
            products[at, k * LANES : (k + 1) * LANES] = value

        tap_products(lambda x, y: load(x, y, at), lambda x, y: gradient(x, y, at), rows, keep)
        return carry

    lax.fori_loop(0, channels // GROUP, step, 0)
    return jnp.dot(products[...], selector[...], preferred_element_type=F32)


def fetch(source, target, sem):
    copy = pltpu.make_async_copy(source, target, sem)
    copy.start()
    return copy


def rows_of(value, wide, rows):
    for group in range(value.shape[0] // GROUP):
        at = group_rows(group)
        wide[...] = value[at].astype(F32).reshape(GROUP * 8, LANES)
        for row in range(8):
            rows[row, at, :] = wide[pl.ds(row, GROUP, stride=8), :].astype(BF)


def slab_at(index, channels):
    return pl.ds(index * channels, channels)


def density_kernel(
    own_ref, value_far, dw_one_far, dw_two_far, pw_one_far, pw_two_far, rows, strip, rest, rest_more,
    value, dw_one, dw_two, pw_one, pw_two, wide, sems,
):
    own = own_ref[0]
    moves = ((value_far, value), (dw_one_far, dw_one), (dw_two_far, dw_two), (pw_one_far, pw_one), (pw_two_far, pw_two))
    copies = [fetch(source, target, sems.at[index]) for index, (source, target) in enumerate(moves)]
    for copy in copies:
        copy.wait()
    channels = value.shape[0]
    rows_of(value, wide, rows)
    for x in range(2):
        for y in range(2):
            strip[slab_at(x * 2 + y, channels), :] = rows[x * 4 + 2 * own + y]
            piece = rows[x * 4 + 2 - 2 * own + y]
            rest[slab_at(x * 2 + y, channels), :] = piece
            rest_more[slab_at(x * 2 + y, channels), :] = piece
    base = 4 * channels
    strip[base:, :] = jnp.zeros((64, LANES), BF)
    strip[base : base + 27, :] = dw_one[...]
    strip[base + 32 : base + 59, :] = dw_two[...]
    half = channels // 2
    for index, weight in enumerate((pw_one, pw_two)):
        for side in range(2):
            start = base + index * channels + side * half
            rest_more[start : start + half, :] = weight[:, side * LANES : (side + 1) * LANES]


def cotangent_kernel(own_ref, value_far, rows, strip, rest, value, wide, sem):
    own = own_ref[0]
    fetch(value_far, value, sem).wait()
    channels = value.shape[0]
    rows_of(value, wide, rows)
    for x in range(2):
        for y in range(2):
            strip[slab_at(x * 2 + y, channels), :] = rows[x * 4 + 2 * own + y]
            rest[slab_at(x * 2 + y, channels), :] = rows[x * 4 + 2 - 2 * own + y]


def weights_kernel(own_ref, mine, message, weight_one, weight_two, weight_one_t):
    first = own_ref[0] == 0
    channels = weight_one.shape[0]
    half = channels // 2
    base = 4 * channels
    for index, out in enumerate((weight_one, weight_two)):
        start = base + index * channels
        here, other = (
            side_by_side([part[start : start + half, :], part[start + half : start + channels, :]]).astype(F32) for part in (mine, message)
        )
        top, bottom = jnp.where(first, here, other), jnp.where(first, other, here)
        out[:half, :] = top.astype(BF)
        out[half:, :] = bottom.astype(BF)
        if index == 0:
            weight_one_t[:, :half] = top.T.astype(BF)
            weight_one_t[:, half:] = bottom.T.astype(BF)


def stencil_kernel(
    own_ref, mine, message, one_forward, one_back, two_forward, two_back, turn, selector, columns, stencils, sems
):
    first = own_ref[0] == 0
    here, there = (part[part.shape[0] - 64 :, :].astype(F32) for part in (mine, message))
    columns[...] = side_by_side([jnp.where(first, here, there), jnp.where(first, there, here)]).T
    channels = columns.shape[0]
    outs = (one_forward, one_back, two_forward, two_back)
    row = lax.broadcasted_iota(jnp.int32, (GROUP, LANES), 0)
    lane = lax.broadcasted_iota(jnp.int32, (GROUP, LANES), 1)
    diagonal = lane % GROUP == row
    masks = [jnp.logical_and(diagonal, (lane // GROUP) % 4 == j) for j in range(4)]
    low = lane < 4 * GROUP
    zero = jnp.zeros((GROUP, LANES), F32)

    def step(group, carry):
        at = pl.ds(pl.multiple_of(group * GROUP, GROUP), GROUP)
        block = columns[at, :]
        for base, which in ((0, (0, 1)), (32, (2, 3))):
            wide = [jnp.broadcast_to(block[:, base + k : base + k + 1], (GROUP, LANES)) for k in range(27)]
            for index, sign in zip(which, (1, -1)):
                for d in (-1, 0, 1):
                    for y in range(2):
                        strips = {2: zero}
                        for a in (-1, 0, 1):
                            value = zero
                            for b in (-1, 0, 1):
                                value = jnp.where(masks[y + 1 + b], wide[tap_index(sign * a, sign * b, sign * d)], value)
                            strips[a] = value
                        for x in range(PLANES):
                            for half in range(2):
                                left = (2 * half - x + 1) % 4 - 1
                                right = (2 * half + 1 - x + 1) % 4 - 1
                                tile = jnp.where(low, strips[left], strips[right]).astype(BF)
                                start = (d + 1) * 2 * LANES + half * LANES
                                stencils[index, group, (x * 2 + y) * GROUP : (x * 2 + y + 1) * GROUP, start : start + LANES] = tile
        for index, out in enumerate(outs):
            pltpu.make_async_copy(stencils.at[index, group], out.at[group], sems.at[index]).start()
        return carry

    lax.fori_loop(0, channels // GROUP, step, 0)
    source = lax.broadcasted_iota(jnp.int32, (LANES, LANES), 0)
    target = lax.broadcasted_iota(jnp.int32, (LANES, LANES), 1)
    turn[:, :LANES] = (source == (target + LANES - 1) % LANES).astype(F32).astype(BF)
    turn[:, LANES:] = (source == (target + 1) % LANES).astype(F32).astype(BF)
    for k in range(27):
        selector[k * LANES : (k + 1) * LANES, :] = (target == k).astype(F32).astype(BF)
    for index, out in enumerate(outs):
        pltpu.make_async_copy(stencils.at[index], out, sems.at[index]).wait()


def fill_extended(own, ext, local, beside, rest, halo, halo_beside):
    channels = local.shape[1]
    for x in range(2):
        for y in range(4):
            ext[x * 6 + 2 * (1 - own) + y] = local[x * 4 + y]
        for y in range(2):
            at = slab_at(x * 2 + y, channels)
            ext[x * 6 + 4 * own + y] = halo[at, :]
            ext[(x + 2) * 6 + 4 * own + y] = halo_beside[at, :]
            ext[(x + 2) * 6 + 2 + y] = beside[at, :]
            ext[(x + 2) * 6 + 4 * (1 - own) + y] = rest[at, :]


def forward_kernel(
    own_ref, one_source, two_source, local, beside, rest, halo, halo_beside, turn, weight_t, ext, first, act, slope, second,
    one_forward, two_forward, one_sem, two_sem, moved,
):
    channels = local.shape[1]
    one_copy, two_copy = fetch(one_source, one_forward, one_sem), fetch(two_source, two_forward, two_sem)
    fill_extended(own_ref[0], ext, local, beside, rest, halo, halo_beside)
    one_copy.wait()

    def emit(x, y, rows, total):
        first[x * 4 + y, rows, :] = total.astype(BF)

    stencil_sums(ext, one_forward, turn, moved, 2, emit)
    for base in range(0, 16, 4):
        source = side_by_side([first[base + j] for j in range(4)])
        pre = jnp.dot(weight_t[...], source, preferred_element_type=F32)
        sigma = jax.nn.sigmoid(pre)
        value = (pre * sigma).astype(BF)
        factor = (sigma * (1.0 + pre * (1.0 - sigma))).astype(BF)
        for j in range(4):
            act[base + j] = value[:, j * LANES : (j + 1) * LANES]
            slope[base + j] = factor[:, j * LANES : (j + 1) * LANES]

    two_copy.wait()

    def emit_second(x, y, rows, total):
        second[x * 2 + y, rows, :] = total.astype(BF)

    stencil_sums(act, two_forward, turn, moved, 1, emit_second)


def second_kernel(own_ref, act, second, local, beside, weight, selector, grad_pw, grad_dw, cotan, grad_second, products):
    own = own_ref[0]
    channels = act.shape[1]
    for x in range(2):
        for y in range(2):
            cotan[x * 2 + y] = local[x * 4 + 2 * own + y]
            cotan[(x + 2) * 2 + y] = beside[slab_at(x * 2 + y, channels), :]
    for x in range(PLANES):
        source = side_by_side([cotan[x * 2], cotan[x * 2 + 1]])
        value = jnp.dot(weight[...], source, preferred_element_type=F32).astype(BF)
        grad_second[x * 2] = value[:, :LANES]
        grad_second[x * 2 + 1] = value[:, LANES:]
    total = jnp.zeros((channels, channels), F32)
    for x in range(PLANES):
        total += contract(side_by_side([second[2 * x], second[2 * x + 1]]), side_by_side([cotan[2 * x], cotan[2 * x + 1]]))
    grad_pw[...] = total
    grad_dw[...] = tap_sums(
        lambda x, y, rows: act[x * 4 + y, rows, :], lambda x, y, rows: grad_second[x * 2 + y - 1, rows, :], range(1, 3), products, selector
    )


def backward_kernel(
    own_ref, core_ref, two_source, local, beside, rest, halo, halo_beside, slope, first, density, turn, weight_two, weight_one,
    selector, grad_pw_two, grad_dw_two, grad_first, parts, ext, grad_second, grad_pre, products, whole, two_back, two_sem, moved,
):
    core = core_ref[0]
    two_copy = fetch(two_source, two_back, two_sem)
    channels = local.shape[1]
    half = channels // 2
    fill_extended(own_ref[0], ext, local, beside, rest, halo, halo_beside)
    for base in range(0, 24, 4):
        source = side_by_side([ext[base + j] for j in range(4)])
        value = jnp.dot(weight_two[...], source, preferred_element_type=F32).astype(BF)
        for j in range(4):
            grad_second[base + j] = value[:, j * LANES : (j + 1) * LANES]

    two_copy.wait()

    def emit(x, y, rows, total):
        slab = x * 4 + y
        grad_pre[slab, rows, :] = (total * slope[slab, rows, :].astype(F32)).astype(BF)

    stencil_sums(grad_second, two_back, turn, moved, 2, emit)
    for base in range(0, 16, 4):
        source = side_by_side([grad_pre[base + j] for j in range(4)])
        value = jnp.dot(weight_one[...], source, preferred_element_type=F32).astype(BF)
        for j in range(4):
            grad_first[base + j] = value[:, j * LANES : (j + 1) * LANES]
    total = jnp.zeros((channels, channels), F32)
    for x in range(PLANES):
        total += contract(
            side_by_side([first[4 * x + 1], first[4 * x + 2]]), side_by_side([grad_pre[4 * x + 1], grad_pre[4 * x + 2]])
        )
    grad_dw_one = tap_sums(
        lambda x, y, rows: density[x * 6 + y, rows, :], lambda x, y, rows: grad_first[x * 4 + y - 1, rows, :], range(2, 4), products, selector
    )
    dw_one_rows = grad_dw_one.T
    dw_two_rows = grad_dw_two[...].T
    for side in range(2):
        span = slice(side * half, (side + 1) * half)
        whole[side, :half, :] = total[span]
        whole[side, half : 2 * half, :] = grad_pw_two[span, :]
        whole[side, 2 * half :, :half] = dw_one_rows[:32, span]
        whole[side, 2 * half :, half:] = dw_two_rows[:32, span]
    block = parts.shape[2]
    for part in range(2):
        place = part * (1 - core) + (1 - part) * core
        parts[place] = whole[:, part * block : (part + 1) * block, :]


def input_kernel(own_ref, one_source, local, beside, grad_first, turn, mine, other, one_back, one_sem, moved):
    own = own_ref[0]
    fetch(one_source, one_back, one_sem).wait()
    channels = local.shape[1]

    def emit(x, y, rows, total):
        slab = (x % 2) * 2 + y
        if x < 2:
            mine[slab, rows, :] = (local[x * 4 + 2 * own + y, rows, :].astype(F32) + total).astype(BF)
        else:
            at = pl.ds(slab * channels + rows.start, GROUP)
            other[slab, rows, :] = (beside[at, :].astype(F32) + total).astype(BF)

    stencil_sums(grad_first, one_back, turn, moved, 1, emit)


def finish_kernel(scale, core_ref, mine, other, pw_one, pw_two, dw_one, dw_two):
    first = core_ref[0] == 0
    top = jnp.where(first, mine[...], other[...]) * scale
    bottom = jnp.where(first, other[...], mine[...]) * scale
    half = pw_one.shape[0]
    spare = top.shape[0] - half
    pw_one[...] = top[:half]
    pw_two[:spare, :] = top[half:]
    pw_two[spare:, :] = bottom[: half - spare]
    dw_one[...] = bottom[half - spare : half - spare + 27, :half]
    dw_two[...] = bottom[half - spare : half - spare + 27, half:]


def call(kernel, name, outs, scratch, scalars, inputs, limit, far_in=(), far_out=0):
    return pl.pallas_call(
        kernel,
        name=name,
        out_shape=[(pltpu.HBM if i < far_out else jax.ShapeDtypeStruct)(shape, dtype) for i, (shape, dtype) in enumerate(outs)],
        in_specs=[SMEM] * len(scalars) + [HBM] * len(far_in) + [VMEM] * len(inputs),
        out_specs=[HBM] * far_out + [VMEM] * (len(outs) - far_out),
        scratch_shapes=scratch,
        compiler_params=pltpu.CompilerParams(vmem_limit_bytes=limit * 1024 * 1024),
        cost_estimate=pl.CostEstimate(flops=MICROSECONDS[name] * 1_150_000_000, bytes_accessed=1024, transcendentals=0),
    )(*scalars, *[pltpu.with_memory_space_constraint(value, pltpu.HBM) for value in far_in], *inputs)


def shards(density, cotangent, pw_one, pw_two, dw_one, dw_two):
    channels, extent_x, extent_y, extent_z = density.shape
    own_size, space_size = lax.axis_size("own"), lax.axis_size("space")
    own, spot = lax.axis_index("own"), lax.axis_index("space")
    core = spot % 2
    place = lambda o, s: o * space_size + s % space_size
    every = [(o, s) for o in range(own_size) for s in range(space_size)]
    across = [(place(o, s), place(1 - o, s)) for o, s in every]
    onward = [(place(o, s), place(o, s + 1 - 2 * o)) for o, s in every]
    swap = lambda value: lax.ppermute(value, AXES, across)
    pass_on = lambda value: lax.ppermute(value, AXES, onward)
    own_ref = own.astype(jnp.int32).reshape(1)
    core_ref = core.astype(jnp.int32).reshape(1)

    slab = (channels, LANES)

    merged = lambda value: value.reshape(channels, extent_x * extent_y, extent_z)
    wide = pltpu.VMEM((GROUP * 8, LANES), F32)
    whole = pltpu.VMEM((channels, extent_x * extent_y, extent_z), BF)
    density_rows, density_strip, density_rest, density_rest_more = call(
        density_kernel, "density",
        [((8,) + slab, BF), ((4 * channels + 64, LANES), BF), ((4 * channels, LANES), BF), ((6 * channels, LANES), BF)],
        [whole] + [pltpu.VMEM(part.shape, BF) for part in (dw_one, dw_two, pw_one, pw_two)] + [wide, pltpu.SemaphoreType.DMA((5,))],
        (own_ref,), (), 16, far_in=(merged(density), dw_one, dw_two, pw_one, pw_two),
    )
    cot_rows, cot_strip, cot_rest = call(
        cotangent_kernel, "cotangent",
        [((8,) + slab, BF), ((4 * channels, LANES), BF), ((4 * channels, LANES), BF)],
        [whole, wide, pltpu.SemaphoreType.DMA],
        (own_ref,), (), 16, far_in=(merged(cotangent),),
    )
    density_far = swap(density_strip)
    density_beside = swap(density_rest_more)
    density_rest, cot_strip, cot_rest = lax.optimization_barrier((density_rest, cot_strip, cot_rest))
    cot_far = swap(cot_strip)
    density_halo = pass_on(density_rest)
    cot_halo = pass_on(cot_rest)
    density_far, cot_rest = lax.optimization_barrier((density_far, cot_rest))
    density_halo_far = pass_on(density_far)
    cot_beside = swap(cot_rest)
    weight_one, weight_two, weight_one_t = call(
        weights_kernel, "weights", [((channels, channels), BF)] * 3, [],
        (own_ref,), (density_rest_more, density_beside), 16,
    )

    stencil = (channels // GROUP, 8 * GROUP, 48 * GROUP)
    held = pltpu.VMEM(stencil, BF)
    sem = pltpu.SemaphoreType.DMA
    moved = pltpu.VMEM((2, 24) + slab, BF)
    products = pltpu.VMEM((channels, 27 * LANES), BF)
    some = lambda count: pltpu.VMEM((count,) + slab, BF)
    one_forward, one_back, two_forward, two_back, turn, selector = call(
        stencil_kernel, "stencils",
        [(stencil, BF)] * 4 + [((LANES, 2 * LANES), BF), ((27 * LANES, LANES), BF)],
        [pltpu.VMEM((channels, 64), F32), pltpu.VMEM((4,) + stencil, BF), pltpu.SemaphoreType.DMA((4,))],
        (own_ref,), (density_strip, density_far), 32, far_out=4,
    )
    density_ext, first, act, slope, second = call(
        forward_kernel, "forward",
        [((24,) + slab, BF)] + [((16,) + slab, BF)] * 3 + [((8,) + slab, BF)],
        [held, held, sem, sem, moved],
        (own_ref,),
        (density_rows, density_beside, density_far, density_halo, density_halo_far, turn, weight_one_t),
        40, far_in=(one_forward, two_forward),
    )
    cot_far, act = lax.optimization_barrier((cot_far, act))
    cot_halo_far = pass_on(cot_far)
    pw_two_part, dw_two_part = call(
        second_kernel, "second",
        [((channels, channels), F32), ((channels, LANES), F32)],
        [some(8), some(8), products],
        (own_ref,), (act, second, cot_rows, cot_beside, weight_two, selector),
        32,
    )
    block = (channels + 32) // 2
    grad_first, parts = call(
        backward_kernel, "backward",
        [((16,) + slab, BF), ((2, 2, block, channels), F32)],
        [some(24), some(24), some(16), products, pltpu.VMEM((2, 2 * block, channels), F32), held, sem, moved],
        (own_ref, core_ref),
        (cot_rows, cot_beside, cot_far, cot_halo, cot_halo_far, slope, first, density_ext, turn, weight_two, weight_one,
         selector, pw_two_part, dw_two_part),
        40, far_in=(two_back,),
    )
    twin = [(place(o, s), place(o, s ^ 1)) for o, s in every]
    total = parts[0] + lax.ppermute(parts[1], AXES, twin)
    keep = lax.dynamic_index_in_dim(total, own, 0, keepdims=False)
    give = lax.dynamic_index_in_dim(total, 1 - own, 0, keepdims=False)
    mine, other = call(
        input_kernel, "input",
        [((4,) + slab, BF), ((4,) + slab, BF)], [held, sem, moved],
        (own_ref,), (cot_rows, cot_beside, grad_first, turn),
        32, far_in=(one_back,),
    )
    give, other = lax.optimization_barrier((give.astype(BF), other))
    total = keep + swap(give).astype(F32)
    back = swap(other)
    bits = [1 << i for i in range(1, space_size.bit_length() - 1)]
    swapped = list(bits)
    for i in range(0, len(bits) - 1, 2):
        swapped[i], swapped[i + 1] = bits[i + 1], bits[i]
    for even, odd in zip(bits, swapped):
        pairs = [(place(o, s), place(o, s ^ (odd if s % 2 else even))) for o, s in every]
        sent = total.astype(BF)
        total = sent.astype(F32) + lax.ppermute(sent, AXES, pairs).astype(F32)
    back = back.reshape(2, 2, channels, extent_z)
    mine = mine.reshape(2, 2, channels, extent_z)
    rows = jnp.where(own == 0, jnp.concatenate([mine, back], 1), jnp.concatenate([back, mine], 1))
    total, grad_input = lax.optimization_barrier((total, rows.transpose(2, 0, 1, 3)))
    partner = lax.ppermute(total, AXES, twin)
    scale = 1.0 / math.sqrt(float(extent_x * extent_y * extent_z * own_size * space_size))
    half = channels // 2
    grad_pw_one, grad_pw_two, grad_dw_one, grad_dw_two = call(
        lambda *refs: finish_kernel(scale, *refs), "finish",
        [((half, channels), F32)] * 2 + [((27, half), F32)] * 2, [],
        (core_ref,), (total, partner), 8,
    )
    return grad_input, grad_pw_one, grad_pw_two, grad_dw_one, grad_dw_two


def solution(mesh):
    in_specs = (
        P(None, "own", "space", None),
        P(None, "own", "space", None),
        P("own", None),
        P("own", None),
        P(None, "own"),
        P(None, "own"),
    )
    out_specs = (
        P(None, "own", "space", None),
        P("own", None),
        P("own", None),
        P(None, "own"),
        P(None, "own"),
    )
    return jax.shard_map(shards, mesh=mesh, in_specs=in_specs, out_specs=out_specs, check_vma=False)
```

```python
import math

import jax
import jax.numpy as jnp
from jax import lax
from jax.experimental import pallas as pl
from jax.experimental.pallas import tpu as pltpu
from jax.sharding import PartitionSpec as P

AXES = ("own", "space")
BF = jnp.bfloat16
F32 = jnp.float32
TAPS = [
    (9 * (a + 1) + 3 * (b + 1) + (d + 1), a, b, d)
    for a in (-1, 0, 1)
    for b in (-1, 0, 1)
    for d in (-1, 0, 1)
]
LANES = 128
GROUP = 16
MICROSECONDS = {"density": 1, "cotangent": 1, "weights": 1, "stencils": 5, "forward": 0, "later": 0, "second": 4, "backward": 8, "input": 3, "finish": 1, "assemble": 0}
PLANES = 4
VMEM = pl.BlockSpec(memory_space=pltpu.VMEM)
SMEM = pl.BlockSpec(memory_space=pltpu.SMEM)
HBM = pl.BlockSpec(memory_space=pltpu.HBM)


def tap_index(a, b, d):
    return 9 * (a + 1) + 3 * (b + 1) + (d + 1)


def tree(terms):
    while len(terms) > 1:
        paired = [terms[i] + terms[i + 1] for i in range(0, len(terms) - 1, 2)]
        terms = paired + ([terms[-1]] if len(terms) % 2 else [])
    return terms[0]


def turned(value, shift):
    return pltpu.roll(value, shift % LANES, 1)


def side_by_side(slabs):
    return jnp.concatenate(slabs, axis=1)


def contract(left, right):
    return lax.dot_general(left, right, (((1,), (1,)), ((), ())), preferred_element_type=F32)


def group_rows(group):
    return pl.ds(group * GROUP, GROUP)


def stencil_sums(data, stencil, turn, moved, blocks, emit):
    height = 2 * blocks + 2
    for slab in range(PLANES * height):
        both = jnp.dot(data[slab], turn[...], preferred_element_type=F32).astype(BF)
        moved[0, slab] = both[:, :LANES]
        moved[1, slab] = both[:, LANES:]
    for group in range(data.shape[1] // GROUP):
        rows = group_rows(group)

        def piece(d, x, y):
            return data[x * height + y, rows, :] if d == 1 else moved[d // 2, x * height + y, rows, :]

        columns = [
            jnp.concatenate([piece(d, x, 2 * block + y) for d in range(3) for x in range(PLANES) for y in range(4)], axis=0)
            for block in range(blocks)
        ]
        total = jnp.dot(stencil[group], side_by_side(columns), preferred_element_type=F32)
        for x in range(PLANES):
            for block in range(blocks):
                for y in range(2):
                    start = (x * 2 + y) * GROUP
                    emit(x, 2 * block + y, rows, total[start : start + GROUP, block * LANES : (block + 1) * LANES])


def tap_products(load, gradient, rows, emit):
    turns = {}
    for x in range(PLANES):
        for y in rows:
            wide = gradient(x, y).astype(F32)
            turns[x, y] = {-1: turned(wide, -1), 0: wide, 1: turned(wide, 1)}
    for k, a, b, d in TAPS:
        emit(k, tree([load((x + a) % PLANES, y + b).astype(F32) * turns[x, y][d] for x in range(PLANES) for y in rows]))


def tap_sums(load, gradient, rows, products, selector):
    channels = products.shape[0]

    def step(group, carry):
        at = pl.ds(pl.multiple_of(group * GROUP, GROUP), GROUP)

        def keep(k, value):
            products[at, k * LANES : (k + 1) * LANES] = value.astype(BF)

        tap_products(lambda x, y: load(x, y, at), lambda x, y: gradient(x, y, at), rows, keep)
        return carry

    lax.fori_loop(0, channels // GROUP, step, 0)
    return jnp.dot(products[...], selector[...], preferred_element_type=F32)


def fetch(source, target, sem):
    copy = pltpu.make_async_copy(source, target, sem)
    copy.start()
    return copy


def rows_of(value, wide, rows):
    for group in range(value.shape[0] // GROUP):
        at = group_rows(group)
        wide[...] = value[at].astype(F32).reshape(GROUP * 8, LANES)
        for row in range(8):
            rows[row, at, :] = wide[pl.ds(row, GROUP, stride=8), :].astype(BF)


def slab_at(index, channels):
    return pl.ds(index * channels, channels)


def density_kernel(
    own_ref, core_ref, value_far, dw_one_far, dw_two_far, pw_one_far, pw_two_far, rows, strip, rest, rest_more, weights,
    value, dw_one, dw_two, pw_one, pw_two, wide, sems,
):
    own = own_ref[0]
    moves = ((value_far, value), (dw_one_far, dw_one), (dw_two_far, dw_two), (pw_one_far, pw_one), (pw_two_far, pw_two))
    copies = [fetch(source, target, sems.at[index]) for index, (source, target) in enumerate(moves)]
    for copy in copies:
        copy.wait()
    channels = value.shape[0]
    rows_of(value, wide, rows)
    for x in range(2):
        for y in range(2):
            strip[slab_at(x * 2 + y, channels), :] = rows[x * 4 + 2 * own + y]
            piece = rows[x * 4 + 2 - 2 * own + y]
            rest[slab_at(x * 2 + y, channels), :] = piece
            rest_more[slab_at(x * 2 + y, channels), :] = piece
    base = 4 * channels
    strip[base:, :] = jnp.zeros((64, LANES), BF)
    strip[base : base + 27, :] = dw_one[...]
    strip[base + 32 : base + 59, :] = dw_two[...]
    half = channels // 2
    for index, weight in enumerate((pw_one, pw_two)):
        for side in range(2):
            start = index * channels + side * half
            weights[start : start + half, :] = weight[:, side * LANES : (side + 1) * LANES]
    rest_more[base:, :] = weights[pl.ds(core_ref[0] * channels, channels), :]


def cotangent_kernel(own_ref, value_far, more, rows, message, rest, value, wide, sem):
    own = own_ref[0]
    copy = fetch(value_far, value, sem)
    channels = value.shape[0]
    message[4 * channels :, :] = more[...]
    copy.wait()
    rows_of(value, wide, rows)
    for x in range(2):
        for y in range(2):
            message[slab_at(x * 2 + y, channels), :] = rows[x * 4 + 2 * own + y]
            rest[slab_at(x * 2 + y, channels), :] = rows[x * 4 + 2 - 2 * own + y]


def weights_kernel(own_ref, core_ref, mine, beside, twin, weight_one, weight_two, weight_one_t):
    first = own_ref[0] == 0
    straight = core_ref[0] == 0
    channels = weight_one.shape[0]
    half = channels // 2
    for index, out in enumerate((weight_one, weight_two)):
        a, b = (part[...].astype(F32) for part in ((beside, twin) if index == 0 else (twin, beside)))
        here, other = (
            side_by_side([part[:half], part[half:]])
            for part in (mine[index * channels : (index + 1) * channels, :].astype(F32), jnp.where(straight, a, b))
        )
        top, bottom = jnp.where(first, here, other), jnp.where(first, other, here)
        out[:half, :] = top.astype(BF)
        out[half:, :] = bottom.astype(BF)
        if index == 0:
            weight_one_t[:, :half] = top.T.astype(BF)
            weight_one_t[:, half:] = bottom.T.astype(BF)


def stencil_kernel(
    own_ref, mine, message, one_back, two_back, one_forward, two_forward, turn, selector, columns, stencils, sems
):
    first = own_ref[0] == 0
    here, there = (part[part.shape[0] - 64 :, :].astype(F32) for part in (mine, message))
    columns[...] = side_by_side([jnp.where(first, here, there), jnp.where(first, there, here)]).T
    channels = columns.shape[0]
    outs = (one_back, two_back)
    targets = [one_forward, two_forward] + [stencils.at[index] for index in range(2)]
    row = lax.broadcasted_iota(jnp.int32, (GROUP, LANES), 0)
    lane = lax.broadcasted_iota(jnp.int32, (GROUP, LANES), 1)
    diagonal = lane % GROUP == row
    masks = [jnp.logical_and(diagonal, (lane // GROUP) % 4 == j) for j in range(4)]
    low = lane < 4 * GROUP
    zero = jnp.zeros((GROUP, LANES), F32)

    def step(group, carry):
        at = pl.ds(pl.multiple_of(group * GROUP, GROUP), GROUP)
        block = columns[at, :]
        for base, which in ((0, (0, 2)), (32, (1, 3))):
            wide = [jnp.broadcast_to(block[:, base + k : base + k + 1], (GROUP, LANES)) for k in range(27)]
            for index, sign in zip(which, (1, -1)):
                for d in (-1, 0, 1):
                    for y in range(2):
                        strips = {2: zero}
                        for a in (-1, 0, 1):
                            value = zero
                            for b in (-1, 0, 1):
                                value = jnp.where(masks[y + 1 + b], wide[tap_index(sign * a, sign * b, sign * d)], value)
                            strips[a] = value
                        for x in range(PLANES):
                            for half in range(2):
                                left = (2 * half - x + 1) % 4 - 1
                                right = (2 * half + 1 - x + 1) % 4 - 1
                                tile = jnp.where(low, strips[left], strips[right]).astype(BF)
                                start = (d + 1) * 2 * LANES + half * LANES
                                targets[index][group, (x * 2 + y) * GROUP : (x * 2 + y + 1) * GROUP, start : start + LANES] = tile
        for index, out in enumerate(outs):
            pltpu.make_async_copy(stencils.at[index, group], out.at[group], sems.at[index]).start()
        return carry

    lax.fori_loop(0, channels // GROUP, step, 0)
    source = lax.broadcasted_iota(jnp.int32, (LANES, LANES), 0)
    target = lax.broadcasted_iota(jnp.int32, (LANES, LANES), 1)
    turn[:, :LANES] = (source == (target + LANES - 1) % LANES).astype(F32).astype(BF)
    turn[:, LANES:] = (source == (target + 1) % LANES).astype(F32).astype(BF)
    for k in range(27):
        selector[k * LANES : (k + 1) * LANES, :] = (target == k).astype(F32).astype(BF)
    for index, out in enumerate(outs):
        pltpu.make_async_copy(stencils.at[index], out, sems.at[index]).wait()


def fill_extended(own, ext, local, beside, rest, halo, halo_beside, beside_base=0):
    channels = local.shape[1]
    for x in range(2):
        for y in range(4):
            ext[x * 6 + 2 * (1 - own) + y] = local[x * 4 + y]
        for y in range(2):
            at = slab_at(x * 2 + y, channels)
            ext[x * 6 + 4 * own + y] = halo[at, :]
            ext[(x + 2) * 6 + 4 * own + y] = halo_beside[at, :]
            ext[(x + 2) * 6 + 2 + y] = beside[pl.ds(beside_base + (x * 2 + y) * channels, channels), :]
            ext[(x + 2) * 6 + 4 * (1 - own) + y] = rest[at, :]


def forward_kernel(
    own_ref, local, beside, rest, halo, halo_beside, one_forward, turn, weight_t, ext, first, act, slope, moved
):
    fill_extended(own_ref[0], ext, local, beside, rest, halo, halo_beside, beside_base=4 * local.shape[1])

    def emit(x, y, rows, total):
        first[x * 4 + y, rows, :] = total.astype(BF)

    stencil_sums(ext, one_forward, turn, moved, 2, emit)
    for base in range(0, 16, 4):
        source = side_by_side([first[base + j] for j in range(4)])
        pre = jnp.dot(weight_t[...], source, preferred_element_type=F32)
        sigma = 0.5 * jnp.tanh(0.5 * pre) + 0.5
        value = (pre * sigma).astype(BF)
        factor = (sigma * (1.0 + pre * (1.0 - sigma))).astype(BF)
        for j in range(4):
            act[base + j] = value[:, j * LANES : (j + 1) * LANES]
            slope[base + j] = factor[:, j * LANES : (j + 1) * LANES]


def later_kernel(act, two_forward, turn, second, moved):

    def emit(x, y, rows, total):
        second[x * 2 + y, rows, :] = total.astype(BF)

    stencil_sums(act, two_forward, turn, moved, 1, emit)


def second_kernel(own_ref, act, second, local, beside, weight, selector, grad_pw, grad_dw, cotan, grad_second, products):
    own = own_ref[0]
    channels = act.shape[1]
    for x in range(2):
        for y in range(2):
            cotan[x * 2 + y] = local[x * 4 + 2 * own + y]
            cotan[(x + 2) * 2 + y] = beside[slab_at(x * 2 + y, channels), :]
    for x in range(PLANES):
        source = side_by_side([cotan[x * 2], cotan[x * 2 + 1]])
        value = jnp.dot(weight[...], source, preferred_element_type=F32).astype(BF)
        grad_second[x * 2] = value[:, :LANES]
        grad_second[x * 2 + 1] = value[:, LANES:]
    total = jnp.zeros((channels, channels), F32)
    for x in range(PLANES):
        total += contract(side_by_side([second[2 * x], second[2 * x + 1]]), side_by_side([cotan[2 * x], cotan[2 * x + 1]]))
    grad_pw[...] = total
    grad_dw[...] = tap_sums(
        lambda x, y, rows: act[x * 4 + y, rows, :], lambda x, y, rows: grad_second[x * 2 + y - 1, rows, :], range(1, 3), products, selector
    )


def backward_kernel(
    own_ref, core_ref, two_source, local, beside, rest, halo, halo_beside, slope, first, density, turn, weight_two, weight_one,
    selector, grad_pw_two, grad_dw_two, grad_first, parts, ext, grad_second, grad_pre, products, whole, two_back, two_sem, moved,
):
    core = core_ref[0]
    two_copy = fetch(two_source, two_back, two_sem)
    channels = local.shape[1]
    half = channels // 2
    fill_extended(own_ref[0], ext, local, beside, rest, halo, halo_beside)
    for base in range(0, 24, 4):
        source = side_by_side([ext[base + j] for j in range(4)])
        value = jnp.dot(weight_two[...], source, preferred_element_type=F32).astype(BF)
        for j in range(4):
            grad_second[base + j] = value[:, j * LANES : (j + 1) * LANES]

    two_copy.wait()

    def emit(x, y, rows, total):
        slab = x * 4 + y
        grad_pre[slab, rows, :] = (total * slope[slab, rows, :].astype(F32)).astype(BF)

    stencil_sums(grad_second, two_back, turn, moved, 2, emit)
    for base in range(0, 16, 4):
        source = side_by_side([grad_pre[base + j] for j in range(4)])
        value = jnp.dot(weight_one[...], source, preferred_element_type=F32).astype(BF)
        for j in range(4):
            grad_first[base + j] = value[:, j * LANES : (j + 1) * LANES]
    total = jnp.zeros((channels, channels), F32)
    for x in range(PLANES):
        total += contract(
            side_by_side([first[4 * x + 1], first[4 * x + 2]]), side_by_side([grad_pre[4 * x + 1], grad_pre[4 * x + 2]])
        )
    grad_dw_one = tap_sums(
        lambda x, y, rows: density[x * 6 + y, rows, :], lambda x, y, rows: grad_first[x * 4 + y - 1, rows, :], range(2, 4), products, selector
    )
    dw_one_rows = grad_dw_one.T
    dw_two_rows = grad_dw_two[...].T
    for side in range(2):
        span = slice(side * half, (side + 1) * half)
        whole[side, :half, :] = total[span]
        whole[side, half : 2 * half, :] = grad_pw_two[span, :]
        whole[side, 2 * half :, :half] = dw_one_rows[:32, span]
        whole[side, 2 * half :, half:] = dw_two_rows[:32, span]
    block = parts.shape[2]
    for part in range(2):
        place = part * (1 - core) + (1 - part) * core
        parts[place] = whole[:, part * block : (part + 1) * block, :]


def input_kernel(own_ref, one_source, local, beside, grad_first, turn, mine, other, one_back, one_sem, moved):
    own = own_ref[0]
    fetch(one_source, one_back, one_sem).wait()
    channels = local.shape[1]

    def emit(x, y, rows, total):
        slab = (x % 2) * 2 + y
        if x < 2:
            mine[slab, rows, :] = (local[x * 4 + 2 * own + y, rows, :].astype(F32) + total).astype(BF)
        else:
            at = pl.ds(slab * channels + rows.start, GROUP)
            other[slab, rows, :] = (beside[at, :].astype(F32) + total).astype(BF)

    stencil_sums(grad_first, one_back, turn, moved, 1, emit)


def assemble_kernel(own_ref, mine, back, out, wide):
    own = own_ref[0]
    channels = out.shape[0]
    for group in range(channels // GROUP):
        at = group_rows(group)
        for x in range(2):
            for y in range(2):
                wide[pl.ds(x * 4 + 2 * own + y, GROUP, stride=8), :] = mine[x * 2 + y, at, :].astype(F32)
                wide[pl.ds(x * 4 + 2 - 2 * own + y, GROUP, stride=8), :] = back[x * 2 + y, at, :].astype(F32)
        out[at] = wide[...].reshape(GROUP, 8, LANES).astype(BF)


def finish_kernel(scale, core_ref, mine, other, pw_one, pw_two, dw_one, dw_two):
    first = core_ref[0] == 0
    top = jnp.where(first, mine[...], other[...]) * scale
    bottom = jnp.where(first, other[...], mine[...]) * scale
    half = pw_one.shape[0]
    spare = top.shape[0] - half
    pw_one[...] = top[:half]
    pw_two[:spare, :] = top[half:]
    pw_two[spare:, :] = bottom[: half - spare]
    dw_one[...] = bottom[half - spare : half - spare + 27, :half]
    dw_two[...] = bottom[half - spare : half - spare + 27, half:]


def call(kernel, name, outs, scratch, scalars, inputs, limit, far_in=(), far_out=0):
    return pl.pallas_call(
        kernel,
        name=name,
        out_shape=[(pltpu.HBM if i < far_out else jax.ShapeDtypeStruct)(shape, dtype) for i, (shape, dtype) in enumerate(outs)],
        in_specs=[SMEM] * len(scalars) + [HBM] * len(far_in) + [VMEM] * len(inputs),
        out_specs=[HBM] * far_out + [VMEM] * (len(outs) - far_out),
        scratch_shapes=scratch,
        compiler_params=pltpu.CompilerParams(vmem_limit_bytes=limit * 1024 * 1024),
        cost_estimate=pl.CostEstimate(flops=MICROSECONDS[name] * 1_150_000_000, bytes_accessed=1024, transcendentals=0),
    )(*scalars, *[pltpu.with_memory_space_constraint(value, pltpu.HBM) for value in far_in], *inputs)


def shards(density, cotangent, pw_one, pw_two, dw_one, dw_two):
    channels, extent_x, extent_y, extent_z = density.shape
    own_size, space_size = lax.axis_size("own"), lax.axis_size("space")
    own, spot = lax.axis_index("own"), lax.axis_index("space")
    core = spot % 2
    place = lambda o, s: o * space_size + s % space_size
    every = [(o, s) for o in range(own_size) for s in range(space_size)]
    across = [(place(o, s), place(1 - o, s)) for o, s in every]
    onward = [(place(o, s), place(o, s + 1 - 2 * o)) for o, s in every]
    swap = lambda value: lax.ppermute(value, AXES, across)
    pass_on = lambda value: lax.ppermute(value, AXES, onward)
    own_ref = own.astype(jnp.int32).reshape(1)
    core_ref = core.astype(jnp.int32).reshape(1)

    slab = (channels, LANES)

    merged = lambda value: value.reshape(channels, extent_x * extent_y, extent_z)
    wide = pltpu.VMEM((GROUP * 8, LANES), F32)
    whole = pltpu.VMEM((channels, extent_x * extent_y, extent_z), BF)
    density_rows, density_strip, density_rest, density_rest_more, pw_mine = call(
        density_kernel, "density",
        [((8,) + slab, BF), ((4 * channels + 64, LANES), BF), ((4 * channels, LANES), BF), ((5 * channels, LANES), BF), ((2 * channels, LANES), BF)],
        [whole] + [pltpu.VMEM(part.shape, BF) for part in (dw_one, dw_two, pw_one, pw_two)] + [wide, pltpu.SemaphoreType.DMA((5,))],
        (own_ref, core_ref), (), 16, far_in=(merged(density), dw_one, dw_two, pw_one, pw_two),
    )
    cot_rows, message, cot_rest = call(
        cotangent_kernel, "cotangent",
        [((8,) + slab, BF), ((9 * channels, LANES), BF), ((4 * channels, LANES), BF)],
        [whole, wide, pltpu.SemaphoreType.DMA],
        (own_ref,), (density_rest_more,), 16, far_in=(merged(cotangent),),
    )
    density_far = swap(density_strip)
    density_rest, message = lax.optimization_barrier((density_rest, message))
    message = swap(message)
    density_halo = pass_on(density_rest)
    density_far, cot_rest = lax.optimization_barrier((density_far, cot_rest))
    density_halo_far = pass_on(density_far)
    cot_beside = swap(cot_rest)
    stencil = (channels // GROUP, 8 * GROUP, 48 * GROUP)
    held = pltpu.VMEM(stencil, BF)
    sem = pltpu.SemaphoreType.DMA
    moved = pltpu.VMEM((2, 24) + slab, BF)
    products = pltpu.VMEM((channels, 27 * LANES), BF)
    some = lambda count: pltpu.VMEM((count,) + slab, BF)
    one_back, two_back, one_forward, two_forward, turn, selector = call(
        stencil_kernel, "stencils",
        [(stencil, BF)] * 4 + [((LANES, 2 * LANES), BF), ((27 * LANES, LANES), BF)],
        [pltpu.VMEM((channels, 64), F32), pltpu.VMEM((2,) + stencil, BF), pltpu.SemaphoreType.DMA((2,))],
        (own_ref,), (density_strip, density_far), 32, far_out=2,
    )
    cot_rest, turn = lax.optimization_barrier((cot_rest, turn))
    message, turn = lax.optimization_barrier((message, turn))
    cot_far = message[: 4 * channels]
    cot_halo_far = pass_on(cot_far)
    cot_halo = pass_on(cot_rest)
    twin = [(place(o, s), place(o, s ^ 1)) for o, s in every]
    pw_beside = message[8 * channels :]
    pw_twin = lax.ppermute(pw_beside, AXES, twin)
    weight_one, weight_two, weight_one_t = call(
        weights_kernel, "weights", [((channels, channels), BF)] * 3, [],
        (own_ref, core_ref), (pw_mine, pw_beside, pw_twin), 16,
    )

    density_ext, first, act, slope = call(
        forward_kernel, "forward",
        [((24,) + slab, BF)] + [((16,) + slab, BF)] * 3, [moved],
        (own_ref,),
        (density_rows, message, density_far, density_halo, density_halo_far, one_forward, turn, weight_one_t),
        40,
    )
    (second,) = call(later_kernel, "later", [((8,) + slab, BF)], [moved], (), (act, two_forward, turn), 32)
    pw_two_part, dw_two_part = call(
        second_kernel, "second",
        [((channels, channels), F32), ((channels, LANES), F32)],
        [some(8), some(8), products],
        (own_ref,), (act, second, cot_rows, cot_beside, weight_two, selector),
        32,
    )
    block = (channels + 32) // 2
    grad_first, parts = call(
        backward_kernel, "backward",
        [((16,) + slab, BF), ((2, 2, block, channels), F32)],
        [some(24), some(24), some(16), products, pltpu.VMEM((2, 2 * block, channels), F32), held, sem, moved],
        (own_ref, core_ref),
        (cot_rows, cot_beside, cot_far, cot_halo, cot_halo_far, slope, first, density_ext, turn, weight_two, weight_one,
         selector, pw_two_part, dw_two_part),
        40, far_in=(two_back,),
    )
    total = parts[0] + lax.ppermute(parts[1], AXES, twin)
    keep = lax.dynamic_index_in_dim(total, own, 0, keepdims=False)
    give = lax.dynamic_index_in_dim(total, 1 - own, 0, keepdims=False)
    total = keep + swap(give.astype(BF)).astype(F32)
    total, grad_first = lax.optimization_barrier((total, grad_first))
    mine, other = call(
        input_kernel, "input",
        [((4,) + slab, BF), ((4,) + slab, BF)], [held, sem, moved],
        (own_ref,), (cot_rows, cot_beside, grad_first, turn),
        32, far_in=(one_back,),
    )
    bits = [1 << i for i in range(1, space_size.bit_length() - 1)]
    swapped = list(bits)
    for i in range(0, len(bits) - 1, 2):
        swapped[i], swapped[i + 1] = bits[i + 1], bits[i]
    for even, odd in zip(bits, swapped):
        pairs = [(place(o, s), place(o, s ^ (odd if s % 2 else even))) for o, s in every]
        sent = total.astype(BF)
        if even == bits[1]:
            sent, other = lax.optimization_barrier((sent, other))
            back = swap(other)
        total = sent.astype(F32) + lax.ppermute(sent, AXES, pairs).astype(F32)
    (grad_input,) = call(
        assemble_kernel, "assemble", [((channels, extent_x * extent_y, extent_z), BF)], [wide], (own_ref,), (mine, back), 16,
    )
    grad_input = grad_input.reshape(density.shape)
    partner = lax.ppermute(total, AXES, twin)
    scale = 1.0 / math.sqrt(float(extent_x * extent_y * extent_z * own_size * space_size))
    half = channels // 2
    grad_pw_one, grad_pw_two, grad_dw_one, grad_dw_two = call(
        lambda *refs: finish_kernel(scale, *refs), "finish",
        [((half, channels), F32)] * 2 + [((27, half), F32)] * 2, [],
        (core_ref,), (total, partner), 8,
    )
    return grad_input, grad_pw_one, grad_pw_two, grad_dw_one, grad_dw_two


def solution(mesh):
    in_specs = (
        P(None, "own", "space", None),
        P(None, "own", "space", None),
        P("own", None),
        P("own", None),
        P(None, "own"),
        P(None, "own"),
    )
    out_specs = (
        P(None, "own", "space", None),
        P("own", None),
        P("own", None),
        P(None, "own"),
        P(None, "own"),
    )
    return jax.shard_map(shards, mesh=mesh, in_specs=in_specs, out_specs=out_specs, check_vma=False)
```
